32 devices in a mesh: ctx: 8 (over z, y), head: 4 (over x, core).
Axes of the slice: x: 2, y: 2, z: 4, core: 2. Of those that a mesh axis runs over, the one named last changes fastest.
Arguments:
- latents: float32 [512, 1024], replicated, may hold values from -5 to 5
- observations: float32 [16384, 1024], P('ctx'), may hold values from -45 to 45
- w_query: float32 [1024, 1024], P(None, 'head'), as said below
- w_key: float32 [1024, 1024], P(None, 'head'), as said below
- w_value: float32 [1024, 1024], P(None, 'head'), may hold values from -0.1875 to 0.1875
- w_out: float32 [1024, 1024], P('head'), may hold values from -0.1875 to 0.1875
- d_out: float32 [512, 1024], replicated, may hold values from -6 to 6
Outputs:
- d_latents: float32 [512, 1024], P(None, 'head')
- d_observations: float32 [16384, 1024], P('ctx', 'head')
- d_w_query: float32 [1024, 1024], P(None, 'head')
- d_w_key: float32 [1024, 1024], P('ctx', 'head')
- d_w_value: float32 [1024, 1024], P('ctx', 'head')
- d_w_out: float32 [1024, 1024], P('head')
The draws below stay inside these ranges and needn't reach their ends.
Inputs may be any that keep to these rules, and one draw needn't show every extreme that they name: `w_query`: every entry lies within -5 / sqrt(1024) to 5 / sqrt(1024). `w_key`: every entry lies within -7 / sqrt(1024) to 7 / sqrt(1024).
All inputs are finite; a program needn't handle non-finite values.
Results may differ from the reference program's by a relative error of at most 0.0003.
Values sent between devices are 32-bit elements; how exact they have to be, the bound alone decides.
A program may use at most 128 MiB of HBM per device.

```python
import math
import jax
import jax.numpy as jnp
from jax import lax

D = 1024
HEADS = 8
DH = 128
LAT = 512
TOKENS = 16384


def shared_latents(key):
    return jnp.clip(jax.random.normal(key, (LAT, D), jnp.float32), -5.0, 5.0)


def shared_query(key):
    base = jax.random.normal(jax.random.fold_in(key, 100), (D, HEADS * DH), jnp.float32)
    return jnp.clip(base, -5.0, 5.0) / jnp.sqrt(jnp.float32(D))


def draw_latents(key, part):
    drawn = shared_latents(key)
    return drawn


def draw_observations(key, part):
    key = jax.random.fold_in(key, 2)
    return jnp.clip(jax.random.normal(key, (TOKENS, D), jnp.float32), -5.0, 5.0)


def draw_w_query(key, part):
    return shared_query(key)


def draw_w_key(key, part):
    key = jax.random.fold_in(key, 3)
    own = jnp.clip(jax.random.normal(key, (D, HEADS * DH), jnp.float32), -5.0, 5.0) / jnp.sqrt(jnp.float32(D))
    return own


def levels(own_key, shape, split, least, largest):
    factor_of, own = 1.0, jax.random.fold_in(own_key, 6)
    for dim, parts in split:
        steps = jnp.exp(jax.random.uniform(jax.random.fold_in(own, dim), (parts,), jnp.float32, least / len(split), largest / len(split)))
        factor_of = factor_of * jnp.repeat(steps, shape[dim] // parts).reshape([-1 if axis == dim else 1 for axis in range(len(shape))])
    return factor_of


def bell_draw(rng, dims, scale, reach, shards=(), kind=jnp.bfloat16):
    array = jax.random.normal(rng, dims, jnp.float32) * scale
    if len(shards) > 0:
        array = levels(rng, dims, shards, -0.22, 0.18) * array
    return jnp.clip(array, min=-reach, max=reach).astype(kind)


def setup_inputs(seed: int = 0) -> dict:
    key_of = jax.random.split(jax.random.key(seed), 8)
    return {
        "latents": draw_latents(jax.random.fold_in(key_of[7], 71), 0),
        "observations": draw_observations(jax.random.fold_in(key_of[7], 71), 0),
        "w_query": draw_w_query(jax.random.fold_in(key_of[7], 71), 0),
        "w_key": draw_w_key(jax.random.fold_in(key_of[7], 71), 0),
        "w_value": bell_draw(key_of[4], (D, HEADS * DH), D ** -0.5, 0.1875, ((1, 4),), jnp.float32),
        "w_out": bell_draw(key_of[5], (HEADS * DH, D), (HEADS * DH) ** -0.5, 0.1875, ((0, 4),), jnp.float32),
        "d_out": bell_draw(key_of[6], (LAT, D), 1.0, 6.0, (), jnp.float32),
    }


def reference(latents, observations, w_query, w_key, w_value, w_out, d_out):
    highest = lax.Precision.HIGHEST
    scale = 1.0 / math.sqrt(DH)
    queries = jnp.dot(latents, w_query, precision=highest, preferred_element_type=jnp.float32).reshape(LAT, HEADS, DH)
    keys_all = jnp.dot(observations, w_key, precision=highest, preferred_element_type=jnp.float32).reshape(TOKENS, HEADS, DH)
    values_all = jnp.dot(observations, w_value, precision=highest, preferred_element_type=jnp.float32).reshape(TOKENS, HEADS, DH)
    grad_heads = jnp.dot(d_out, w_out.T, precision=highest, preferred_element_type=jnp.float32).reshape(LAT, HEADS, DH)

    def one_head(pieces):
        query_h, key_h, value_h, grad_h = pieces
        scores = jnp.dot(query_h, key_h.T, precision=highest, preferred_element_type=jnp.float32) * scale
        probs = jnp.exp(scores - lax.optimization_barrier(jnp.max(scores, axis=1, keepdims=True)))
        probs = probs / lax.optimization_barrier(jnp.sum(probs, axis=1, keepdims=True))
        attended = jnp.dot(probs, value_h, precision=highest, preferred_element_type=jnp.float32)
        dprobs = jnp.dot(grad_h, value_h.T, precision=highest, preferred_element_type=jnp.float32)
        delta = lax.optimization_barrier(jnp.sum(grad_h * attended, axis=1, keepdims=True))
        dscores = probs * (dprobs - delta) * scale
        dquery = jnp.dot(dscores, key_h, precision=highest, preferred_element_type=jnp.float32)
        dkey = jnp.dot(dscores.T, query_h, precision=highest, preferred_element_type=jnp.float32)
        dvalue = jnp.dot(probs.T, grad_h, precision=highest, preferred_element_type=jnp.float32)
        return (attended, dquery, dkey, dvalue)
    stacked = (jnp.transpose(queries, (1, 0, 2)), jnp.transpose(keys_all, (1, 0, 2)), jnp.transpose(values_all, (1, 0, 2)), jnp.transpose(grad_heads, (1, 0, 2)))
    attended, dquery, dkey, dvalue = lax.map(one_head, stacked)
    attended = jnp.transpose(attended, (1, 0, 2)).reshape(LAT, HEADS * DH)
    dquery = jnp.transpose(dquery, (1, 0, 2)).reshape(LAT, HEADS * DH)
    dkey = jnp.transpose(dkey, (1, 0, 2)).reshape(TOKENS, HEADS * DH)
    dvalue = jnp.transpose(dvalue, (1, 0, 2)).reshape(TOKENS, HEADS * DH)
    d_w_out = jnp.dot(attended.T, d_out, precision=highest, preferred_element_type=jnp.float32)
    d_latents = jnp.dot(dquery, w_query.T, precision=highest, preferred_element_type=jnp.float32)
    d_w_query = jnp.dot(latents.T, dquery, precision=highest, preferred_element_type=jnp.float32)
    d_observations = jnp.dot(dkey, w_key.T, precision=highest, preferred_element_type=jnp.float32) + jnp.dot(dvalue, w_value.T, precision=highest, preferred_element_type=jnp.float32)
    d_w_key = jnp.dot(observations.T, dkey, precision=highest, preferred_element_type=jnp.float32)
    d_w_value = jnp.dot(observations.T, dvalue, precision=highest, preferred_element_type=jnp.float32)
    return (d_latents, d_observations, d_w_query, d_w_key, d_w_value, d_w_out)
```

```python
import math

import jax
import jax.numpy as jnp
from jax import lax
from jax.sharding import PartitionSpec as P

DH = 128


def on_device(latents, observations, w_query, w_key, w_value, w_out, d_out):
    high = lax.Precision.HIGH

    def mm(spec, a, b):
        return jnp.einsum(spec, a, b, precision=high, preferred_element_type=jnp.float32)

    scale = 1.0 / math.sqrt(DH)
    lat_rows = latents.shape[0]
    tok_rows = observations.shape[0]
    width_here = w_query.shape[1]
    heads_here = width_here // DH
    queries = mm("ld,dw->lw", latents, w_query).reshape(lat_rows, heads_here, DH)
    grad_heads = mm("ld,wd->lw", d_out, w_out).reshape(lat_rows, heads_here, DH)
    keys_here = mm("td,dw->tw", observations, w_key).reshape(tok_rows, heads_here, DH)
    values_here = mm("td,dw->tw", observations, w_value).reshape(tok_rows, heads_here, DH)
    scores = mm("lhd,thd->hlt", queries, keys_here) * scale
    dprobs = mm("lhd,thd->hlt", grad_heads, values_here)
    row_max = jnp.max(scores, axis=2)
    expo = jnp.exp(scores - row_max[..., None])
    stats = jnp.stack([row_max, jnp.sum(expo, axis=2), jnp.sum(expo * dprobs, axis=2)])
    all_stats = lax.all_gather(stats, "ctx")
    top = jnp.max(all_stats[:, 0], axis=0)
    weight = jnp.exp(all_stats[:, 0] - top)
    total = jnp.sum(weight * all_stats[:, 1], axis=0)
    delta = jnp.sum(weight * all_stats[:, 2], axis=0) / total
    probs = expo * (jnp.exp(row_max - top) / total)[..., None]
    dscores = probs * (dprobs - delta[..., None]) * scale
    dkey = mm("hlt,lhd->thd", dscores, queries).reshape(tok_rows, width_here)
    dvalue = mm("hlt,lhd->thd", probs, grad_heads).reshape(tok_rows, width_here)
    token_part = mm("tw,dw->td", dkey, w_key) + mm("tw,dw->td", dvalue, w_value)
    d_observations = lax.psum_scatter(token_part, "head", scatter_dimension=1, tiled=True)
    joined = jnp.concatenate([dkey, dvalue], axis=1)
    mine = lax.psum_scatter(
        mm("td,tw->dw", observations, joined), "ctx", scatter_dimension=0, tiled=True
    )
    attended_part = mm("hlt,thd->lhd", probs, values_here).reshape(lat_rows, width_here)
    dquery_part = mm("hlt,thd->lhd", dscores, keys_here).reshape(lat_rows, width_here)
    attended, dquery = lax.psum((attended_part, dquery_part), "ctx")
    d_w_out = mm("lw,ld->wd", attended, d_out)
    d_w_query = mm("ld,lw->dw", latents, dquery)
    latent_part = mm("lw,dw->ld", dquery, w_query)
    d_latents = lax.psum_scatter(latent_part, "head", scatter_dimension=1, tiled=True)
    d_w_key = mine[:, :width_here]
    d_w_value = mine[:, width_here:]
    return (d_latents, d_observations, d_w_query, d_w_key, d_w_value, d_w_out)


def solution(mesh):
    placed = (
        P(),
        P("ctx", None),
        P(None, "head"),
        P(None, "head"),
        P(None, "head"),
        P("head", None),
        P(),
    )
    return jax.shard_map(
        on_device,
        mesh=mesh,
        in_specs=placed,
        out_specs=(
            P(None, "head"),
            P("ctx", "head"),
            P(None, "head"),
            P("ctx", "head"),
            P("ctx", "head"),
            P("head", None),
        ),
        check_vma=False,
    )
```

```python
import functools
import math

import jax
import jax.numpy as jnp
from jax import lax
from jax.experimental import pallas as pl
from jax.experimental.pallas import tpu as pltpu
from jax.sharding import PartitionSpec as P

DH = 128
CORES = 2
F32 = jnp.float32
BF16 = jnp.bfloat16
MESH = pl.DeviceIdType.MESH
STD = (((1,), (0,)), ((), ()))
RHS_T = (((1,), (1,)), ((), ()))


def split(x):
    hi = x.astype(BF16)
    return hi, (x - hi.astype(F32)).astype(BF16)


def dot(a, b, dims=STD):
    return lax.dot_general(a, b, dims, preferred_element_type=F32)


def dot3(a, b, dims=STD):
    (ah, al), (bh, bl) = a, b
    return dot(ah, bh, dims) + (dot(ah, bl, dims) + dot(al, bh, dims))


def wide_left(x):
    hi, lo = split(x)
    return jnp.concatenate([hi, hi, lo, lo], axis=1)


def wide_right(x):
    hi, lo = split(x)
    return jnp.concatenate([hi, lo, hi, lo], axis=1)


def narrow_dot(a, b_pair, b_hi):
    hi, lo = split(a)
    both = dot(hi, b_pair)
    return both[:, :DH] + (both[:, DH:] + dot(lo, b_hi))


def short_dot(a_t, b):
    ah, al = split(a_t)
    bh, bl = split(b)
    both = dot(jnp.concatenate([ah, al], axis=0), bh)
    return both[:DH] + (both[DH:] + dot(ah, bl))


def kernel(
    cfg,
    lat, obs, wq, wk, wv, wo, dout,
    dlat_o, dobs_o, dwq_o, dwk_o, dwv_o, dwo_o,
    expo, dprob, kv, obuf, wh, wl, q4, g4, qp, gp, stat, rstat, acc,
    one_recv, x_recv,
    dw, dw1, dw2, ab, ab1, ab2, db, db1, db2, aall, dall, lall, wqr, hbuf,
    obs_sem, st_s, st_r, wq_s, wq_r, h_s, h_r, t1_s, t1_r, tx_s, tx_r,
    y_s, y_r, z_s, z_r,
):
    NC, NH, NY, TC = cfg
    NZ, NX = NC // NY, NH // CORES
    T, D = obs.shape
    L, W = lat.shape[0], wq.shape[1]
    H, NCH, blk, la = W // DH, T // TC, D // NH, L // NC
    scale = 1.0 / math.sqrt(DH)
    ctx, head = lax.axis_index("ctx"), lax.axis_index("head")
    z, y = ctx // NY, lax.rem(ctx, NY)
    x, core = head // CORES, lax.rem(head, CORES)

    def other(me, k, n):
        return lax.rem(me + k, n)

    barrier = pltpu.get_barrier_semaphore()
    for k in range(1, NC):
        pl.semaphore_signal(barrier, inc=1, device_id=(other(ctx, k, NC), head), device_id_type=MESH)
    for k in range(1, NH):
        pl.semaphore_signal(barrier, inc=1, device_id=(ctx, other(head, k, NH)), device_id_type=MESH)

    def fetch(i):
        s = lax.rem(i, 2)
        return pltpu.make_async_copy(obs.at[pl.ds(pl.multiple_of(i * TC, TC), TC)], obuf.at[s], obs_sem.at[s])

    def remote(src, dst, ss, rs, dev):
        return pltpu.make_async_remote_copy(
            src_ref=src, dst_ref=dst, send_sem=ss, recv_sem=rs, device_id=dev, device_id_type=MESH
        )

    fetch(0).start()
    for half, w in ((0, wk), (1, wv)):
        hi, lo = split(w[...])
        wh[:, half * W:(half + 1) * W] = hi
        wl[:, half * W:(half + 1) * W] = lo
    q = dot3(split(lat[...]), split(wq[...])) * scale
    g = dot3(split(dout[...]), split(wo[...]), RHS_T)
    for h in range(H):
        for full, wide, pair in ((q, q4, qp), (g, g4, gp)):
            piece = full[:, h * DH:(h + 1) * DH]
            wide[h] = wide_right(piece)
            pair[h] = jnp.concatenate(split(piece), axis=1)
    pl.semaphore_wait(barrier, NC + NH - 2)

    wq_copies = [
        remote(
            wq.at[pl.ds(pl.multiple_of(other(head, k, NH) * blk, blk), blk)], wqr.at[k],
            wq_s.at[k], wq_r.at[k], (ctx, other(head, k, NH)),
        )
        for k in range(1, NH)
    ]
    for c in wq_copies:
        c.start()

    def rows(i):
        return pl.ds(pl.multiple_of(i * TC, TC), TC)

    def scores_step(i, tops):
        @pl.when(i + 1 < NCH)
        def _():
            fetch(i + 1).start()

        fetch(i).wait()
        o = split(obuf[lax.rem(i, 2)])
        both = dot3(o, (wh[...], wl[...]))
        kv[i] = both
        out = []
        for h in range(H):
            s = dot(wide_left(both[:, h * DH:(h + 1) * DH]), q4[h], RHS_T)
            expo[h, rows(i)] = s
            out.append(jnp.maximum(tops[h], jnp.max(s, axis=0, keepdims=True)))
            dprob[h, rows(i)] = dot(wide_left(both[:, W + h * DH:W + (h + 1) * DH]), g4[h], RHS_T)
        return tuple(out)

    tops = lax.fori_loop(0, NCH, scores_step, tuple(jnp.full((1, L), -3e38, F32) for _ in range(H)))
    fetch(0).start()

    def exp_step(i, sums):
        out = []
        for h in range(H):
            e = jnp.exp(expo[h, rows(i)] - tops[h])
            expo[h, rows(i)] = e
            out.append(sums[2 * h] + jnp.sum(e, axis=0, keepdims=True))
            out.append(sums[2 * h + 1] + jnp.sum(e * dprob[h, rows(i)], axis=0, keepdims=True))
        return tuple(out)

    sums = lax.fori_loop(0, NCH, exp_step, tuple(jnp.zeros((1, L), F32) for _ in range(2 * H)))
    stat[...] = jnp.zeros_like(stat)
    for h in range(H):
        stat[3 * h:3 * h + 1] = tops[h]
        stat[3 * h + 1:3 * h + 2] = sums[2 * h]
        stat[3 * h + 2:3 * h + 3] = sums[2 * h + 1]
    st_copies = [
        remote(stat, rstat.at[k], st_s.at[k], st_r.at[k], (other(ctx, k, NC), head)) for k in range(1, NC)
    ]
    for c in st_copies:
        c.start()

    acc[...] = jnp.zeros_like(acc)

    def acc_step(i, _):
        both = kv[i]
        for h in range(H):
            v_t = both[:, W + h * DH:W + (h + 1) * DH].T
            acc[h * DH:(h + 1) * DH] += short_dot(v_t, expo[h, rows(i)])
        return 0

    lax.fori_loop(0, NCH, acc_step, 0)

    for c in st_copies:
        c.wait()
    weights, deltas = [], []
    for h in range(H):
        top = tops[h]
        for k in range(1, NC):
            top = jnp.maximum(top, rstat[k, 3 * h:3 * h + 1])
        mine = jnp.exp(tops[h] - top)
        total, cross = mine * sums[2 * h], mine * sums[2 * h + 1]
        for k in range(1, NC):
            theirs = jnp.exp(rstat[k, 3 * h:3 * h + 1] - top)
            total += theirs * rstat[k, 3 * h + 1:3 * h + 2]
            cross += theirs * rstat[k, 3 * h + 2:3 * h + 3]
        weights.append(mine / total)
        deltas.append(cross / total)

    def sum_y(buf, got, n):
        return [
            remote(buf.at[:, other(y, k, NY)], got.at[k], y_s.at[n, k], y_r.at[n, k], (z * NY + other(y, k, NY), head))
            for k in range(1, NY)
        ]

    def sum_z(buf, got, n):
        return [
            remote(buf.at[other(z, k, NZ), y], got.at[k], z_s.at[n, k], z_r.at[n, k], (other(z, k, NZ) * NY + y, head))
            for k in range(1, NZ)
        ]

    def all_z(buf, n):
        return [
            remote(buf.at[z, y], buf.at[z, y], z_s.at[n, k], z_r.at[n, k], (other(z, k, NZ) * NY + y, head))
            for k in range(1, NZ)
        ]

    def all_y(buf, n):
        return [
            remote(buf.at[:, y], buf.at[:, y], y_s.at[n, k], y_r.at[n, k], (z * NY + other(y, k, NY), head))
            for k in range(1, NY)
        ]

    def start(copies):
        for c in copies:
            c.start()
        return copies

    def wait(copies):
        for c in copies:
            c.wait()

    def add_y(buf, got):
        total = buf[:, pl.ds(y, 1)]
        for k in range(1, NY):
            total += got[k].reshape(total.shape)
        buf[:, pl.ds(y, 1)] = total

    def add_z(buf, got):
        total = buf[pl.ds(z, 1), pl.ds(y, 1)].reshape(got.shape[1:])
        for k in range(1, NZ):
            total += got[k]
        return total

    def put(buf, value):
        buf[pl.ds(z, 1), pl.ds(y, 1)] = value.reshape((1, 1) + value.shape)

    for h in range(H):
        ab[:, :, :, h * DH:(h + 1) * DH] = (acc[h * DH:(h + 1) * DH] * weights[h]).T.reshape(NZ, NY, la, DH)
    att_y = start(sum_y(ab, ab1, 0))

    acc[...] = jnp.zeros_like(acc)
    dw[...] = jnp.zeros_like(dw)

    def grad_step(i, _):
        @pl.when(i + 1 < NCH)
        def _():
            fetch(i + 1).start()

        fetch(i).wait()
        both = kv[i]
        dk, dv = [], []
        for h in range(H):
            p = expo[h, rows(i)] * weights[h]
            ds = p * (dprob[h, rows(i)] - deltas[h])
            dk.append(narrow_dot(ds, qp[h], qp[h, :, :DH]))
            dv.append(narrow_dot(p, gp[h], gp[h, :, :DH]))
            acc[h * DH:(h + 1) * DH] += short_dot(both[:, h * DH:(h + 1) * DH].T, ds)
        both = jnp.concatenate(dk + dv, axis=1)
        kv[i] = both
        o_t = obuf[lax.rem(i, 2)].T
        dw[...] += dot3(split(o_t), split(both)).reshape(dw.shape)
        return 0

    lax.fori_loop(0, NCH, grad_step, 0)
    for h in range(H):
        db[:, :, :, h * DH:(h + 1) * DH] = (acc[h * DH:(h + 1) * DH] * scale).T.reshape(NZ, NY, la, DH)
    dq_y = start(sum_y(db, db1, 1))
    dw_y = start(sum_y(dw, dw1, 2))

    partner = (ctx, x * CORES + (1 - core))

    def first(i):
        return remote(dprob.at[0, rows(i)], one_recv.at[rows(i)], t1_s.at[i], t1_r.at[i], partner)

    def second(i, k):
        xp = other(x, k, NX)
        cols = pl.ds(pl.multiple_of(xp * blk, blk), blk)
        return remote(
            expo.at[0, rows(i), cols], x_recv.at[k - 1, rows(i)], tx_s.at[k, i], tx_r.at[k, i],
            (ctx, xp * CORES + core),
        )

    def forward(i):
        first(i).wait_recv()
        expo[0, rows(i)] += one_recv[rows(i)]
        for k in range(1, NX):
            second(i, k).start()

    def token_step(i, _):
        grads = split(kv[i])
        for xp in range(NX):
            b = pl.ds(pl.multiple_of((xp * CORES + (1 - core)) * blk, blk), blk)
            dprob[0, rows(i), xp * blk:(xp + 1) * blk] = dot3(grads, (wh[b], wl[b]), RHS_T)
        first(i).start()
        for xp in range(NX):
            b = pl.ds(pl.multiple_of((xp * CORES + core) * blk, blk), blk)
            expo[0, rows(i), xp * blk:(xp + 1) * blk] = dot3(grads, (wh[b], wl[b]), RHS_T)

        @pl.when(i > 0)
        def _():
            forward(i - 1)

        return 0

    quarter = NCH // 4
    lax.fori_loop(0, quarter, token_step, 0)
    wait(att_y)
    add_y(ab, ab1)
    att_z = start(sum_z(ab, ab2, 0))
    wait(dq_y)
    add_y(db, db1)
    dq_z = start(sum_z(db, db2, 1))

    lax.fori_loop(quarter, 2 * quarter, token_step, 0)
    wait(att_z)
    put(aall, add_z(ab, ab2))
    att_az = start(all_z(aall, 2))
    wait(dq_z)
    dq_mine = add_z(db, db2)
    put(dall, dq_mine)
    hbuf[0] = dq_mine
    dq_az = start(all_z(dall, 3))
    dq_h = start([
        remote(hbuf.at[0], hbuf.at[k], h_s.at[k], h_r.at[k], (ctx, other(head, k, NH))) for k in range(1, NH)
    ])

    lax.fori_loop(2 * quarter, 3 * quarter, token_step, 0)
    wait(att_az)
    att_ay = start(all_y(aall, 3))
    wait(dq_az)
    dq_ay = start(all_y(dall, 4))
    wait(wq_copies)
    wait(dq_h)
    mine_rows = pl.ds(pl.multiple_of(head * blk, blk), blk)
    lat_part = dot3(split(hbuf[0]), split(wq[mine_rows]), RHS_T)
    for k in range(1, NH):
        lat_part += dot3(split(hbuf[k]), split(wqr[k]), RHS_T)
    put(lall, lat_part)
    lat_az = start(all_z(lall, 4))
    wait(dw_y)
    add_y(dw, dw1)
    dw_z = start(sum_z(dw, dw2, 5))

    lax.fori_loop(3 * quarter, NCH, token_step, 0)
    forward(NCH - 1)
    wait(lat_az)
    lat_ay = start(all_y(lall, 5))
    wait(att_ay)
    att_t = aall[...].reshape(L, W).T
    dwo_o[...] = dot3(split(att_t), split(dout[...]))
    wait(dq_ay)
    dq_t = dall[...].reshape(L, W).T
    dwq_o[...] = dot3(split(dq_t), split(lat[...])).T
    wait(lat_ay)
    dlat_o[...] = lall[...].reshape(L, blk)

    def finish(i, _):
        cols = pl.ds(pl.multiple_of(x * blk, blk), blk)
        total = expo[0, rows(i), cols]
        for k in range(1, NX):
            second(i, k).wait_recv()
            total += x_recv[k - 1, rows(i)]
        dobs_o[rows(i)] = total
        first(i).wait_send()
        for k in range(1, NX):
            second(i, k).wait_send()
        return 0

    lax.fori_loop(0, NCH, finish, 0)
    wait(dw_z)
    dw_mine = add_z(dw, dw2)
    dwk_o[...] = dw_mine[:, :W]
    dwv_o[...] = dw_mine[:, W:]


def on_device(nc, nh, latents, observations, w_query, w_key, w_value, w_out, d_out):
    L, D = latents.shape
    T = observations.shape[0]
    W = w_query.shape[1]
    H, blk, la, r = W // DH, D // nh, L // nc, D // nc
    ny = 1 << ((nc.bit_length() - 1) // 2)
    nz, nx = nc // ny, nh // CORES
    tc = min(256, T // 4)
    nch = T // tc
    stat_rows = -(-3 * H // 8) * 8

    def vm(*shape, dtype=F32):
        return pltpu.VMEM(shape, dtype)

    def sems(*shape):
        return pltpu.SemaphoreType.DMA(shape)

    vmem = pl.BlockSpec(memory_space=pltpu.VMEM)
    out = lambda *s: jax.ShapeDtypeStruct(s, F32)
    return pl.pallas_call(
        functools.partial(kernel, (nc, nh, ny, tc)),
        out_shape=(out(L, blk), out(T, blk), out(D, W), out(r, W), out(r, W), out(W, D)),
        in_specs=[vmem, pl.BlockSpec(memory_space=pl.ANY)] + [vmem] * 5,
        out_specs=tuple([vmem] * 6),
        scratch_shapes=[
            vm(H, T, L), vm(H, T, L), vm(nch, tc, 2 * W), vm(2, tc, D),
            vm(D, 2 * W, dtype=BF16), vm(D, 2 * W, dtype=BF16),
            vm(H, L, 4 * DH, dtype=BF16), vm(H, L, 4 * DH, dtype=BF16),
            vm(H, L, 2 * DH, dtype=BF16), vm(H, L, 2 * DH, dtype=BF16),
            vm(stat_rows, L), vm(nc, stat_rows, L), vm(W, L),
            vm(T, nx * blk), vm(max(nx - 1, 1), T, blk),
            vm(nz, ny, r, 2 * W), vm(ny, nz, r, 2 * W), vm(nz, r, 2 * W),
            vm(nz, ny, la, W), vm(ny, nz, la, W), vm(nz, la, W),
            vm(nz, ny, la, W), vm(ny, nz, la, W), vm(nz, la, W),
            vm(nz, ny, la, W), vm(nz, ny, la, W), vm(nz, ny, la, blk),
            vm(nh, blk, W), vm(nh, la, W),
            sems(2), sems(nc), sems(nc), sems(nh), sems(nh), sems(nh), sems(nh),
            sems(nch), sems(nch), sems(nx, nch), sems(nx, nch),
            sems(6, ny), sems(6, ny), sems(6, nz), sems(6, nz),
        ],
        compiler_params=pltpu.CompilerParams(
            collective_id=0, has_side_effects=True, vmem_limit_bytes=63 * 2**20
        ),
        cost_estimate=pl.CostEstimate(flops=3 * 11 * 10**9, bytes_accessed=40 * 2**20, transcendentals=H * T * L),
    )(latents, observations, w_query, w_key, w_value, w_out, d_out)


def solution(mesh):
    placed = (
        P(),
        P("ctx", None),
        P(None, "head"),
        P(None, "head"),
        P(None, "head"),
        P("head", None),
        P(),
    )
    return jax.shard_map(
        functools.partial(on_device, mesh.shape["ctx"], mesh.shape["head"]),
        mesh=mesh,
        in_specs=placed,
        out_specs=(
            P(None, "head"),
            P("ctx", "head"),
            P(None, "head"),
            P("ctx", "head"),
            P("ctx", "head"),
            P("head", None),
        ),
        check_vma=False,
    )
```

```python
import functools
import math

import jax
import jax.numpy as jnp
from jax import lax
from jax.experimental import pallas as pl
from jax.experimental.pallas import tpu as pltpu
from jax.sharding import PartitionSpec as P

DH = 128
CORES = 2
F32 = jnp.float32
BF16 = jnp.bfloat16
MESH = pl.DeviceIdType.MESH
STD = (((1,), (0,)), ((), ()))
RHS_T = (((1,), (1,)), ((), ()))


def split(x):
    hi = x.astype(BF16)
    return hi, (x - hi.astype(F32)).astype(BF16)


def dot(a, b, dims=STD):
    return lax.dot_general(a, b, dims, preferred_element_type=F32)


def dot3(a, b, dims=STD):
    (ah, al), (bh, bl) = a, b
    return dot(ah, bh, dims) + (dot(ah, bl, dims) + dot(al, bh, dims))


def wide_left(hi, lo):
    return jnp.concatenate([hi, hi, lo, lo], axis=1)


def wide_right(x):
    hi, lo = split(x)
    return jnp.concatenate([hi, lo, hi, lo], axis=1)


def narrow_dot(a, b_pair, b_hi):
    hi, lo = split(a)
    both = dot(hi, b_pair)
    return both[:, :DH] + (both[:, DH:] + dot(lo, b_hi))


def short_dot(hi, lo, b):
    ah = hi.T
    bh, bl = split(b)
    both = dot(jnp.concatenate([ah, lo.T], axis=0), bh)
    return both[:DH] + (both[DH:] + dot(ah, bl))


def kernel(
    cfg,
    lat, obs, wq, wk, wv, wo, dout,
    dlat_o, dobs_o, dq_o, dw_o, att_o,
    expo, dprob, kvh, kvl, obuf, cbuf, wh, wl, q4, g4, qp, gp, stat, rstat, acc,
    one_recv, x_recv,
    dw, dw1, dw2, ab, ab1, ab2, db, db1, db2, aall, dall, lall, wqr, hbuf,
    obs_sem, col_sem, st_s, st_r, wq_s, wq_r, h_s, h_r, t1_s, t1_r, tx_s, tx_r,
    y_s, y_r, z_s, z_r, wy_s, wy_r, wz_s, wz_r, out_sem, res_sem,
):
    NC, NH, NY, TC = cfg
    NZ, NX = NC // NY, NH // CORES
    T, D = obs.shape
    L, W = lat.shape[0], wq.shape[1]
    H, NCH, blk, la, r = W // DH, T // TC, D // NH, L // NC, D // NC
    scale = 1.0 / math.sqrt(DH)
    ctx, head = lax.axis_index("ctx"), lax.axis_index("head")
    z, y = ctx // NY, lax.rem(ctx, NY)
    x, core = head // CORES, lax.rem(head, CORES)

    def other(me, k, n):
        return lax.rem(me + k, n)

    barrier = pltpu.get_barrier_semaphore()
    for k in range(1, NC):
        pl.semaphore_signal(barrier, inc=1, device_id=(other(ctx, k, NC), head), device_id_type=MESH)
    for k in range(1, NH):
        pl.semaphore_signal(barrier, inc=1, device_id=(ctx, other(head, k, NH)), device_id_type=MESH)

    def fetch(i):
        s = lax.rem(i, 2)
        return pltpu.make_async_copy(obs.at[pl.ds(pl.multiple_of(i * TC, TC), TC)], obuf.at[s], obs_sem.at[s])

    def remote(src, dst, ss, rs, dev):
        return pltpu.make_async_remote_copy(
            src_ref=src, dst_ref=dst, send_sem=ss, recv_sem=rs, device_id=dev, device_id_type=MESH
        )

    fetch(0).start()
    for half, w in ((0, wk), (1, wv)):
        hi, lo = split(w[...])
        wh[:, half * W:(half + 1) * W] = hi
        wl[:, half * W:(half + 1) * W] = lo
    q = dot3(split(lat[...]), split(wq[...])) * scale
    g = dot3(split(dout[...]), split(wo[...]), RHS_T)
    for h in range(H):
        for full, wide, pair in ((q, q4, qp), (g, g4, gp)):
            piece = full[:, h * DH:(h + 1) * DH]
            wide[h] = wide_right(piece)
            pair[h] = jnp.concatenate(split(piece), axis=1)
    pl.semaphore_wait(barrier, NC + NH - 2)

    wq_copies = [
        remote(
            wq.at[pl.ds(pl.multiple_of(other(head, k, NH) * blk, blk), blk)], wqr.at[k],
            wq_s.at[k], wq_r.at[k], (ctx, other(head, k, NH)),
        )
        for k in range(1, NH)
    ]
    for c in wq_copies:
        c.start()

    def rows(i):
        return pl.ds(pl.multiple_of(i * TC, TC), TC)

    def scores_step(i, tops):
        @pl.when(i + 1 < NCH)
        def _():
            fetch(i + 1).start()

        fetch(i).wait()
        o = split(obuf[lax.rem(i, 2)])
        both = dot3(o, (wh[...], wl[...]))
        hi, lo = split(both)
        kvh[i] = hi
        kvl[i] = lo
        out = []
        for h in range(H):
            k_h, v_h = slice(h * DH, (h + 1) * DH), slice(W + h * DH, W + (h + 1) * DH)
            s = dot(wide_left(hi[:, k_h], lo[:, k_h]), q4[h], RHS_T)
            expo[h, rows(i)] = s
            out.append(jnp.maximum(tops[h], jnp.max(s, axis=0, keepdims=True)))
            dprob[h, rows(i)] = dot(wide_left(hi[:, v_h], lo[:, v_h]), g4[h], RHS_T)
        return tuple(out)

    tops = lax.fori_loop(0, NCH, scores_step, tuple(jnp.full((1, L), -3e38, F32) for _ in range(H)))

    def fetch_cols(j):
        b = pl.multiple_of(other(z, 1 + j, NZ) * (NY * r), NY * r)
        return pltpu.make_async_copy(obs.at[:, pl.ds(b, NY * r)], cbuf.at[j % 2], col_sem.at[j % 2])

    fetch_cols(0).start()
    if NZ > 1:
        fetch_cols(1).start()

    def exp_step(i, sums):
        out = []
        for h in range(H):
            e = jnp.exp(expo[h, rows(i)] - tops[h])
            expo[h, rows(i)] = e
            out.append(sums[2 * h] + jnp.sum(e, axis=0, keepdims=True))
            out.append(sums[2 * h + 1] + jnp.sum(e * dprob[h, rows(i)], axis=0, keepdims=True))
        return tuple(out)

    sums = lax.fori_loop(0, NCH, exp_step, tuple(jnp.zeros((1, L), F32) for _ in range(2 * H)))
    stat[...] = jnp.zeros_like(stat)
    for h in range(H):
        stat[3 * h:3 * h + 1] = tops[h]
        stat[3 * h + 1:3 * h + 2] = sums[2 * h]
        stat[3 * h + 2:3 * h + 3] = sums[2 * h + 1]
    st_copies = [
        remote(stat, rstat.at[k], st_s.at[k], st_r.at[k], (other(ctx, k, NC), head)) for k in range(1, NC)
    ]
    for c in st_copies:
        c.start()

    acc[...] = jnp.zeros_like(acc)

    def acc_step(i, _):
        for h in range(H):
            v_h = slice(W + h * DH, W + (h + 1) * DH)
            acc[h * DH:(h + 1) * DH] += short_dot(kvh[i, :, v_h], kvl[i, :, v_h], expo[h, rows(i)])
        return 0

    lax.fori_loop(0, NCH, acc_step, 0)

    for c in st_copies:
        c.wait()
    weights, deltas = [], []
    for h in range(H):
        top = tops[h]
        for k in range(1, NC):
            top = jnp.maximum(top, rstat[k, 3 * h:3 * h + 1])
        mine = jnp.exp(tops[h] - top)
        total, cross = mine * sums[2 * h], mine * sums[2 * h + 1]
        for k in range(1, NC):
            theirs = jnp.exp(rstat[k, 3 * h:3 * h + 1] - top)
            total += theirs * rstat[k, 3 * h + 1:3 * h + 2]
            cross += theirs * rstat[k, 3 * h + 2:3 * h + 3]
        weights.append(mine / total)
        deltas.append(cross / total)

    def sum_y(buf, got, n):
        return [
            remote(buf.at[:, other(y, k, NY)], got.at[k], y_s.at[n, k], y_r.at[n, k], (z * NY + other(y, k, NY), head))
            for k in range(1, NY)
        ]

    def sum_z(buf, got, n):
        return [
            remote(buf.at[other(z, k, NZ), y], got.at[k], z_s.at[n, k], z_r.at[n, k], (other(z, k, NZ) * NY + y, head))
            for k in range(1, NZ)
        ]

    def all_z(buf, n):
        return [
            remote(buf.at[z, y], buf.at[z, y], z_s.at[n, k], z_r.at[n, k], (other(z, k, NZ) * NY + y, head))
            for k in range(1, NZ)
        ]

    def all_y(buf, n):
        return [
            remote(buf.at[:, y], buf.at[:, y], y_s.at[n, k], y_r.at[n, k], (z * NY + other(y, k, NY), head))
            for k in range(1, NY)
        ]

    def start(copies):
        for c in copies:
            c.start()
        return copies

    def wait(copies):
        for c in copies:
            c.wait()

    def add_y(buf, got):
        total = buf[:, pl.ds(y, 1)]
        for k in range(1, NY):
            total += got[k].reshape(total.shape)
        buf[:, pl.ds(y, 1)] = total

    def add_z(buf, got):
        total = buf[pl.ds(z, 1), pl.ds(y, 1)].reshape(got.shape[1:])
        for k in range(1, NZ):
            total += got[k]
        return total

    def put(buf, value):
        buf[pl.ds(z, 1), pl.ds(y, 1)] = value.reshape((1, 1) + value.shape)

    for h in range(H):
        ab[:, :, :, h * DH:(h + 1) * DH] = (acc[h * DH:(h + 1) * DH] * weights[h]).T.reshape(NZ, NY, la, DH)
    att_y = start(sum_y(ab, ab1, 0))

    acc[...] = jnp.zeros_like(acc)

    partner = (ctx, x * CORES + (1 - core))

    def first(i):
        return remote(dprob.at[0, rows(i)], one_recv.at[rows(i)], t1_s.at[i], t1_r.at[i], partner)

    def second(i, k):
        xp = other(x, k, NX)
        cols = pl.ds(pl.multiple_of(xp * blk, blk), blk)
        return remote(
            expo.at[0, rows(i), cols], x_recv.at[k - 1, rows(i)], tx_s.at[k, i], tx_r.at[k, i],
            (ctx, xp * CORES + core),
        )

    def forward(i):
        first(i).wait_recv()
        expo[0, rows(i)] += one_recv[rows(i)]
        for k in range(1, NX):
            second(i, k).start()

    def grad_step(i, _):
        dk, dv = [], []
        for h in range(H):
            k_h = slice(h * DH, (h + 1) * DH)
            p = expo[h, rows(i)] * weights[h]
            ds = p * (dprob[h, rows(i)] - deltas[h])
            dk.append(narrow_dot(ds, qp[h], qp[h, :, :DH]))
            dv.append(narrow_dot(p, gp[h], gp[h, :, :DH]))
            acc[h * DH:(h + 1) * DH] += short_dot(kvh[i, :, k_h], kvl[i, :, k_h], ds)
        grads = split(jnp.concatenate(dk + dv, axis=1))
        kvh[i], kvl[i] = grads
        for xp in range(NX):
            b = pl.ds(pl.multiple_of((xp * CORES + (1 - core)) * blk, blk), blk)
            dprob[0, rows(i), xp * blk:(xp + 1) * blk] = dot3(grads, (wh[b], wl[b]), RHS_T)
        first(i).start()
        for xp in range(NX):
            b = pl.ds(pl.multiple_of((xp * CORES + core) * blk, blk), blk)
            expo[0, rows(i), xp * blk:(xp + 1) * blk] = dot3(grads, (wh[b], wl[b]), RHS_T)

        @pl.when(i > 0)
        def _():
            forward(i - 1)

        return 0

    quarter = NCH // 4
    lax.fori_loop(0, quarter, grad_step, 0)
    wait(att_y)
    add_y(ab, ab1)
    att_z = start(sum_z(ab, ab2, 0))
    lax.fori_loop(quarter, 2 * quarter, grad_step, 0)
    wait(att_z)
    put(aall, add_z(ab, ab2))
    att_az = start(all_z(aall, 2))
    lax.fori_loop(2 * quarter, 3 * quarter, grad_step, 0)
    wait(att_az)
    att_ay = start(all_y(aall, 3))
    lax.fori_loop(3 * quarter, NCH, grad_step, 0)
    for h in range(H):
        db[:, :, :, h * DH:(h + 1) * DH] = (acc[h * DH:(h + 1) * DH] * scale).T.reshape(NZ, NY, la, DH)
    pending = {"y": start(sum_y(db, db1, 1))}

    def dq_to_z():
        wait(pending["y"])
        add_y(db, db1)
        pending["z"] = start(sum_z(db, db2, 1))

    def dq_to_all():
        wait(pending["z"])
        mine = add_z(db, db2)
        put(dall, mine)
        hbuf[0] = mine
        pending["az"] = start(all_z(dall, 3))
        pending["h"] = start([
            remote(hbuf.at[0], hbuf.at[k], h_s.at[k], h_r.at[k], (ctx, other(head, k, NH))) for k in range(1, NH)
        ])

    def latents_part():
        wait(pending["az"])
        pending["ay"] = start(all_y(dall, 4))
        wait(wq_copies)
        wait(pending["h"])
        mine_rows = pl.ds(pl.multiple_of(head * blk, blk), blk)
        lat_part = dot3(split(hbuf[0]), split(wq[mine_rows]), RHS_T)
        for k in range(1, NH):
            lat_part += dot3(split(hbuf[k]), split(wqr[k]), RHS_T)
        put(lall, lat_part)
        pending["lat"] = start(all_z(lall, 4))

    stages = [dq_to_z, dq_to_all, latents_part]

    def w_y(j):
        b = other(z, 1 + j, NZ)
        return [
            remote(
                dw.at[b, other(y, k, NY)], dw1.at[k, j], wy_s.at[k, j], wy_r.at[k, j],
                (z * NY + other(y, k, NY), head),
            )
            for k in range(1, NY)
        ]

    def w_z(j):
        b = other(z, 1 + j, NZ)
        return remote(dw.at[b, y], dw2.at[1 + j], wz_s.at[1 + j], wz_r.at[1 + j], (b * NY + y, head))

    def w_sum(j):
        wait(w_y(j))
        b = pl.ds(other(z, 1 + j, NZ), 1)
        total = dw[b, pl.ds(y, 1)]
        for k in range(1, NY):
            total += dw1[k, j].reshape(total.shape)
        dw[b, pl.ds(y, 1)] = total
        if j < NZ - 1:
            w_z(j).start()

    for j in range(NZ):
        fetch_cols(j).wait()
        zb = pl.ds(other(z, 1 + j, NZ), 1)
        dw[zb] = jnp.zeros((1, NY, r, 2 * W), F32)

        def w_step(i, _, j=j, zb=zb):
            o_t = cbuf[j % 2, rows(i)].T
            dw[zb] += dot3(split(o_t), (kvh[i], kvl[i])).reshape(1, NY, r, 2 * W)
            return 0

        lax.fori_loop(0, NCH, w_step, 0)
        if j + 2 < NZ:
            fetch_cols(j + 2).start()
        start(w_y(j))
        if j == 0:
            forward(NCH - 1)
        else:
            w_sum(j - 1)
            if stages:
                stages.pop(0)()
    for stage in stages:
        stage()
    wait(att_ay)
    results = start([pltpu.make_async_copy(aall, att_o, res_sem.at[0])])
    wait(pending["lat"])
    lat_ay = start(all_y(lall, 5))
    wait(pending["ay"])
    results += start([pltpu.make_async_copy(dall, dq_o, res_sem.at[1])])
    w_sum(NZ - 1)
    wait(lat_ay)
    results += start([pltpu.make_async_copy(lall, dlat_o, res_sem.at[2])])

    def out_copy(i):
        cols = pl.ds(pl.multiple_of(x * blk, blk), blk)
        return pltpu.make_async_copy(expo.at[0, rows(i), cols], dobs_o.at[rows(i)], out_sem.at[i])

    def finish(i, _):
        cols = pl.ds(pl.multiple_of(x * blk, blk), blk)
        total = expo[0, rows(i), cols]
        for k in range(1, NX):
            second(i, k).wait_recv()
            total += x_recv[k - 1, rows(i)]
        expo[0, rows(i), cols] = total
        out_copy(i).start()
        first(i).wait_send()
        for k in range(1, NX):
            second(i, k).wait_send()
        return 0

    lax.fori_loop(0, NCH, finish, 0)
    dw_mine = dw[pl.ds(z, 1), pl.ds(y, 1)].reshape(r, 2 * W)
    for j in range(NZ - 1):
        w_z(j).wait()
        dw_mine += dw2[1 + j]
    dw2[0] = dw_mine
    results += start([pltpu.make_async_copy(dw2.at[0], dw_o, res_sem.at[3])])

    def drain(i, _):
        out_copy(i).wait()
        return 0

    lax.fori_loop(0, NCH, drain, 0)
    wait(results)


def last_kernel(att, dq, lat, dout, dlat, dobs, dw, dlat_o, dobs_o, dwq_o, dwk_o, dwv_o, dwo_o, sem):
    W = dq.shape[1]
    moves = [
        pltpu.make_async_copy(dobs, dobs_o, sem.at[0]),
        pltpu.make_async_copy(dlat, dlat_o, sem.at[1]),
        pltpu.make_async_copy(dw.at[:, pl.ds(0, W)], dwk_o, sem.at[2]),
        pltpu.make_async_copy(dw.at[:, pl.ds(W, W)], dwv_o, sem.at[3]),
    ]

    @pl.when(pl.program_id(0) == 0)
    def _():
        for c in moves:
            c.start()

    dwo_o[...] = dot3(split(att[...].T), split(dout[...]))
    dwq_o[...] = dot3(split(lat[...].T), split(dq[...]))

    @pl.when(pl.program_id(0) == pl.num_programs(0) - 1)
    def _():
        for c in moves:
            c.wait()


def on_device(nc, nh, latents, observations, w_query, w_key, w_value, w_out, d_out):
    L, D = latents.shape
    T = observations.shape[0]
    W = w_query.shape[1]
    H, blk, la, r = W // DH, D // nh, L // nc, D // nc
    ny = 1 << ((nc.bit_length() - 1) // 2)
    nz, nx = nc // ny, nh // CORES
    tc = min(256, T // 4)
    nch = T // tc
    stat_rows = -(-3 * H // 8) * 8

    def vm(*shape, dtype=F32):
        return pltpu.VMEM(shape, dtype)

    def sems(*shape):
        return pltpu.SemaphoreType.DMA(shape)

    vmem = pl.BlockSpec(memory_space=pltpu.VMEM)
    out = lambda *s: jax.ShapeDtypeStruct(s, F32)
    anywhere = pl.BlockSpec(memory_space=pl.ANY)
    dlat, dobs, dq, dw, att = pl.pallas_call(
        functools.partial(kernel, (nc, nh, ny, tc)),
        out_shape=(out(nz, ny, la, blk), out(T, blk), out(nz, ny, la, W), out(r, 2 * W), out(nz, ny, la, W)),
        in_specs=[vmem, anywhere] + [vmem] * 5,
        out_specs=(anywhere,) * 5,
        scratch_shapes=[
            vm(H, T, L), vm(H, T, L), vm(nch, tc, 2 * W, dtype=BF16), vm(nch, tc, 2 * W, dtype=BF16),
            vm(2, tc, D), vm(2, T, ny * r),
            vm(D, 2 * W, dtype=BF16), vm(D, 2 * W, dtype=BF16),
            vm(H, L, 4 * DH, dtype=BF16), vm(H, L, 4 * DH, dtype=BF16),
            vm(H, L, 2 * DH, dtype=BF16), vm(H, L, 2 * DH, dtype=BF16),
            vm(stat_rows, L), vm(nc, stat_rows, L), vm(W, L),
            vm(T, nx * blk), vm(max(nx - 1, 1), T, blk),
            vm(nz, ny, r, 2 * W), vm(ny, nz, r, 2 * W), vm(nz, r, 2 * W),
            vm(nz, ny, la, W), vm(ny, nz, la, W), vm(nz, la, W),
            vm(nz, ny, la, W), vm(ny, nz, la, W), vm(nz, la, W),
            vm(nz, ny, la, W), vm(nz, ny, la, W), vm(nz, ny, la, blk),
            vm(nh, blk, W), vm(nh, la, W),
            sems(2), sems(2), sems(nc), sems(nc), sems(nh), sems(nh), sems(nh), sems(nh),
            sems(nch), sems(nch), sems(nx, nch), sems(nx, nch),
            sems(6, ny), sems(6, ny), sems(6, nz), sems(6, nz),
            sems(ny, nz), sems(ny, nz), sems(nz), sems(nz), sems(nch), sems(4),
        ],
        compiler_params=pltpu.CompilerParams(
            collective_id=0, has_side_effects=True, vmem_limit_bytes=63 * 2**20
        ),
        cost_estimate=pl.CostEstimate(flops=3 * 11 * 10**9, bytes_accessed=40 * 2**20, transcendentals=H * T * L),
    )(latents, observations, w_query, w_key, w_value, w_out, d_out)
    wide = D // 4
    whole = pl.BlockSpec((L, W), lambda i: (0, 0))
    columns = pl.BlockSpec((L, wide), lambda i: (0, i))
    return pl.pallas_call(
        last_kernel,
        grid=(4,),
        out_shape=(out(L, blk), out(T, blk), out(D, W), out(r, W), out(r, W), out(W, D)),
        in_specs=[whole, whole, columns, columns, anywhere, anywhere, anywhere],
        out_specs=(
            anywhere, anywhere, pl.BlockSpec((wide, W), lambda i: (i, 0)),
            anywhere, anywhere, pl.BlockSpec((W, wide), lambda i: (0, i)),
        ),
        scratch_shapes=[sems(4)],
        compiler_params=pltpu.CompilerParams(vmem_limit_bytes=62 * 2**20),
        cost_estimate=pl.CostEstimate(flops=12 * L * D * W, bytes_accessed=20 * 2**20, transcendentals=0),
    )(att.reshape(L, W), dq.reshape(L, W), latents, d_out, dlat.reshape(L, blk), dobs, dw)


def solution(mesh):
    placed = (
        P(),
        P("ctx", None),
        P(None, "head"),
        P(None, "head"),
        P(None, "head"),
        P("head", None),
        P(),
    )
    return jax.shard_map(
        functools.partial(on_device, mesh.shape["ctx"], mesh.shape["head"]),
        mesh=mesh,
        in_specs=placed,
        out_specs=(
            P(None, "head"),
            P("ctx", "head"),
            P(None, "head"),
            P("ctx", "head"),
            P("ctx", "head"),
            P("head", None),
        ),
        check_vma=False,
    )
```

```python
import functools
import math

import jax
import jax.numpy as jnp
from jax import lax
from jax.experimental import pallas as pl
from jax.experimental.pallas import tpu as pltpu
from jax.sharding import PartitionSpec as P

DH = 128
CORES = 2
F32 = jnp.float32
BF16 = jnp.bfloat16
MESH = pl.DeviceIdType.MESH
STD = (((1,), (0,)), ((), ()))
RHS_T = (((1,), (1,)), ((), ()))


def split(x):
    hi = x.astype(BF16)
    return hi, (x - hi.astype(F32)).astype(BF16)


def dot(a, b, dims=STD):
    return lax.dot_general(a, b, dims, preferred_element_type=F32)


def dot3(a, b, dims=STD):
    (ah, al), (bh, bl) = a, b
    return dot(ah, bh, dims) + (dot(ah, bl, dims) + dot(al, bh, dims))


def wide_left(x):
    hi, lo = split(x)
    return jnp.concatenate([hi, hi, lo, lo], axis=1)


def wide_right(x):
    hi, lo = split(x)
    return jnp.concatenate([hi, lo, hi, lo], axis=1)


def narrow_dot(a, b_pair, b_hi):
    hi, lo = split(a)
    both = dot(hi, b_pair)
    return both[:, :DH] + (both[:, DH:] + dot(lo, b_hi))


def short_dot(a_t, b):
    ah, al = split(a_t)
    bh, bl = split(b)
    both = dot(jnp.concatenate([ah, al], axis=0), bh)
    return both[:DH] + (both[DH:] + dot(ah, bl))


def kernel(
    cfg,
    lat, obs, wq, wk, wv, wo, dout,
    dlat_o, dobs_o, dq_o, dw_o, att_o,
    expo, dprob, kv, obuf, wh, wl, q4, g4, qp, gp, stat, rstat, acc,
    one_recv, x_recv,
    dw, dw1, dw2, ab, ab1, ab2, db, db1, db2, aall, dall, lall, wqr, hbuf,
    obs_sem, st_s, st_r, wq_s, wq_r, h_s, h_r, t1_s, t1_r, tx_s, tx_r,
    y_s, y_r, z_s, z_r, wy_s, wy_r, wz_s, wz_r, out_sem, res_sem,
):
    NC, NH, NY, TC = cfg
    NZ, NX = NC // NY, NH // CORES
    T, D = obs.shape
    L, W = lat.shape[0], wq.shape[1]
    H, NCH, blk, la, r = W // DH, T // TC, D // NH, L // NC, D // NC
    scale = 1.0 / math.sqrt(DH)
    ctx, head = lax.axis_index("ctx"), lax.axis_index("head")
    z, y = ctx // NY, lax.rem(ctx, NY)
    x, core = head // CORES, lax.rem(head, CORES)

    def other(me, k, n):
        return lax.rem(me + k, n)

    barrier = pltpu.get_barrier_semaphore()
    for k in range(1, NC):
        pl.semaphore_signal(barrier, inc=1, device_id=(other(ctx, k, NC), head), device_id_type=MESH)
    for k in range(1, NH):
        pl.semaphore_signal(barrier, inc=1, device_id=(ctx, other(head, k, NH)), device_id_type=MESH)

    def fetch(i):
        s = lax.rem(i, 2)
        return pltpu.make_async_copy(obs.at[pl.ds(pl.multiple_of(i * TC, TC), TC)], obuf.at[s], obs_sem.at[s])

    def remote(src, dst, ss, rs, dev):
        return pltpu.make_async_remote_copy(
            src_ref=src, dst_ref=dst, send_sem=ss, recv_sem=rs, device_id=dev, device_id_type=MESH
        )

    fetch(0).start()
    for half, w in ((0, wk), (1, wv)):
        hi, lo = split(w[...])
        wh[:, half * W:(half + 1) * W] = hi
        wl[:, half * W:(half + 1) * W] = lo
    q = dot3(split(lat[...]), split(wq[...])) * scale
    g = dot3(split(dout[...]), split(wo[...]), RHS_T)
    for h in range(H):
        for full, wide, pair in ((q, q4, qp), (g, g4, gp)):
            piece = full[:, h * DH:(h + 1) * DH]
            wide[h] = wide_right(piece)
            pair[h] = jnp.concatenate(split(piece), axis=1)
    pl.semaphore_wait(barrier, NC + NH - 2)

    wq_copies = [
        remote(
            wq.at[pl.ds(pl.multiple_of(other(head, k, NH) * blk, blk), blk)], wqr.at[k],
            wq_s.at[k], wq_r.at[k], (ctx, other(head, k, NH)),
        )
        for k in range(1, NH)
    ]
    for c in wq_copies:
        c.start()

    def rows(i):
        return pl.ds(pl.multiple_of(i * TC, TC), TC)

    def scores_step(i, tops):
        @pl.when(i + 1 < NCH)
        def _():
            fetch(i + 1).start()

        fetch(i).wait()
        o = split(obuf[lax.rem(i, 2)])
        both = dot3(o, (wh[...], wl[...]))
        kv[i] = both
        out = []
        for h in range(H):
            s = dot(wide_left(both[:, h * DH:(h + 1) * DH]), q4[h], RHS_T)
            expo[h, rows(i)] = s
            out.append(jnp.maximum(tops[h], jnp.max(s, axis=0, keepdims=True)))
            dprob[h, rows(i)] = dot(wide_left(both[:, W + h * DH:W + (h + 1) * DH]), g4[h], RHS_T)
        return tuple(out)

    tops = lax.fori_loop(0, NCH, scores_step, tuple(jnp.full((1, L), -3e38, F32) for _ in range(H)))
    fetch(0).start()

    def exp_step(i, sums):
        out = []
        for h in range(H):
            e = jnp.exp(expo[h, rows(i)] - tops[h])
            expo[h, rows(i)] = e
            out.append(sums[2 * h] + jnp.sum(e, axis=0, keepdims=True))
            out.append(sums[2 * h + 1] + jnp.sum(e * dprob[h, rows(i)], axis=0, keepdims=True))
        return tuple(out)

    sums = lax.fori_loop(0, NCH, exp_step, tuple(jnp.zeros((1, L), F32) for _ in range(2 * H)))
    stat[...] = jnp.zeros_like(stat)
    for h in range(H):
        stat[3 * h:3 * h + 1] = tops[h]
        stat[3 * h + 1:3 * h + 2] = sums[2 * h]
        stat[3 * h + 2:3 * h + 3] = sums[2 * h + 1]
    st_copies = [
        remote(stat, rstat.at[k], st_s.at[k], st_r.at[k], (other(ctx, k, NC), head)) for k in range(1, NC)
    ]
    for c in st_copies:
        c.start()

    acc[...] = jnp.zeros_like(acc)

    def acc_step(i, _):
        both = kv[i]
        for h in range(H):
            v_t = both[:, W + h * DH:W + (h + 1) * DH].T
            acc[h * DH:(h + 1) * DH] += short_dot(v_t, expo[h, rows(i)])
        return 0

    lax.fori_loop(0, NCH, acc_step, 0)

    for c in st_copies:
        c.wait()
    weights, deltas = [], []
    for h in range(H):
        top = tops[h]
        for k in range(1, NC):
            top = jnp.maximum(top, rstat[k, 3 * h:3 * h + 1])
        mine = jnp.exp(tops[h] - top)
        total, cross = mine * sums[2 * h], mine * sums[2 * h + 1]
        for k in range(1, NC):
            theirs = jnp.exp(rstat[k, 3 * h:3 * h + 1] - top)
            total += theirs * rstat[k, 3 * h + 1:3 * h + 2]
            cross += theirs * rstat[k, 3 * h + 2:3 * h + 3]
        weights.append(mine / total)
        deltas.append(cross / total)

    def sum_y(buf, got, n):
        return [
            remote(buf.at[:, other(y, k, NY)], got.at[k], y_s.at[n, k], y_r.at[n, k], (z * NY + other(y, k, NY), head))
            for k in range(1, NY)
        ]

    def sum_z(buf, got, n):
        return [
            remote(buf.at[other(z, k, NZ), y], got.at[k], z_s.at[n, k], z_r.at[n, k], (other(z, k, NZ) * NY + y, head))
            for k in range(1, NZ)
        ]

    def all_z(buf, n):
        return [
            remote(buf.at[z, y], buf.at[z, y], z_s.at[n, k], z_r.at[n, k], (other(z, k, NZ) * NY + y, head))
            for k in range(1, NZ)
        ]

    def all_y(buf, n):
        return [
            remote(buf.at[:, y], buf.at[:, y], y_s.at[n, k], y_r.at[n, k], (z * NY + other(y, k, NY), head))
            for k in range(1, NY)
        ]

    def start(copies):
        for c in copies:
            c.start()
        return copies

    def wait(copies):
        for c in copies:
            c.wait()

    def add_y(buf, got):
        total = buf[:, pl.ds(y, 1)]
        for k in range(1, NY):
            total += got[k].reshape(total.shape)
        buf[:, pl.ds(y, 1)] = total

    def add_z(buf, got):
        total = buf[pl.ds(z, 1), pl.ds(y, 1)].reshape(got.shape[1:])
        for k in range(1, NZ):
            total += got[k]
        return total

    def put(buf, value):
        buf[pl.ds(z, 1), pl.ds(y, 1)] = value.reshape((1, 1) + value.shape)

    for h in range(H):
        ab[:, :, :, h * DH:(h + 1) * DH] = (acc[h * DH:(h + 1) * DH] * weights[h]).T.reshape(NZ, NY, la, DH)
    att_y = start(sum_y(ab, ab1, 0))

    acc[...] = jnp.zeros_like(acc)
    dw[...] = jnp.zeros_like(dw)

    partner = (ctx, x * CORES + (1 - core))

    def first(i):
        return remote(dprob.at[0, rows(i)], one_recv.at[rows(i)], t1_s.at[i], t1_r.at[i], partner)

    def second(i, k):
        xp = other(x, k, NX)
        cols = pl.ds(pl.multiple_of(xp * blk, blk), blk)
        return remote(
            expo.at[0, rows(i), cols], x_recv.at[k - 1, rows(i)], tx_s.at[k, i], tx_r.at[k, i],
            (ctx, xp * CORES + core),
        )

    def forward(i):
        first(i).wait_recv()
        expo[0, rows(i)] += one_recv[rows(i)]
        for k in range(1, NX):
            second(i, k).start()

    def token_step(i, _):
        grads = split(kv[i])
        for xp in range(NX):
            b = pl.ds(pl.multiple_of((xp * CORES + (1 - core)) * blk, blk), blk)
            dprob[0, rows(i), xp * blk:(xp + 1) * blk] = dot3(grads, (wh[b], wl[b]), RHS_T)
        first(i).start()
        for xp in range(NX):
            b = pl.ds(pl.multiple_of((xp * CORES + core) * blk, blk), blk)
            expo[0, rows(i), xp * blk:(xp + 1) * blk] = dot3(grads, (wh[b], wl[b]), RHS_T)

        @pl.when((i > 0) & (i != NCH // 2))
        def _():
            forward(i - 1)

        return 0

    def grad_step(i, _):
        @pl.when(i + 1 < NCH)
        def _():
            fetch(i + 1).start()

        fetch(i).wait()
        both = kv[i]
        dk, dv = [], []
        for h in range(H):
            p = expo[h, rows(i)] * weights[h]
            ds = p * (dprob[h, rows(i)] - deltas[h])
            dk.append(narrow_dot(ds, qp[h], qp[h, :, :DH]))
            dv.append(narrow_dot(p, gp[h], gp[h, :, :DH]))
            acc[h * DH:(h + 1) * DH] += short_dot(both[:, h * DH:(h + 1) * DH].T, ds)
        both = jnp.concatenate(dk + dv, axis=1)
        kv[i] = both
        o_t = obuf[lax.rem(i, 2)].T
        dw[...] += dot3(split(o_t), split(both)).reshape(dw.shape)
        return 0

    def both_step(i, _):
        grad_step(i, 0)
        token_step(i, 0)
        return 0

    quarter = NCH // 4
    lax.fori_loop(0, quarter, both_step, 0)
    wait(att_y)
    add_y(ab, ab1)
    att_z = start(sum_z(ab, ab2, 0))
    lax.fori_loop(quarter, 2 * quarter, both_step, 0)
    wait(att_z)
    put(aall, add_z(ab, ab2))
    att_az = start(all_z(aall, 2))
    lax.fori_loop(2 * quarter, 3 * quarter, grad_step, 0)
    forward(2 * quarter - 1)
    wait(att_az)
    att_ay = start(all_y(aall, 3))
    lax.fori_loop(3 * quarter, NCH, grad_step, 0)

    def w_y(j):
        b = other(z, 1 + j, NZ)
        return [
            remote(
                dw.at[b, other(y, k, NY)], dw1.at[k, j], wy_s.at[k, j], wy_r.at[k, j],
                (z * NY + other(y, k, NY), head),
            )
            for k in range(1, NY)
        ]

    def w_z(j):
        b = other(z, 1 + j, NZ)
        return remote(dw.at[b, y], dw2.at[1 + j], wz_s.at[1 + j], wz_r.at[1 + j], (b * NY + y, head))

    def w_sum(j):
        wait(w_y(j))
        b = pl.ds(other(z, 1 + j, NZ), 1)
        total = dw[b, pl.ds(y, 1)]
        for k in range(1, NY):
            total += dw1[k, j].reshape(total.shape)
        dw[b, pl.ds(y, 1)] = total
        if j < NZ - 1:
            w_z(j).start()

    for h in range(H):
        db[:, :, :, h * DH:(h + 1) * DH] = (acc[h * DH:(h + 1) * DH] * scale).T.reshape(NZ, NY, la, DH)
    pending = {"y": start(sum_y(db, db1, 1))}

    def dq_to_z():
        wait(pending["y"])
        add_y(db, db1)
        pending["z"] = start(sum_z(db, db2, 1))

    def dq_to_all():
        wait(pending["z"])
        mine = add_z(db, db2)
        put(dall, mine)
        hbuf[0] = mine
        pending["az"] = start(all_z(dall, 3))
        pending["h"] = start([
            remote(hbuf.at[0], hbuf.at[k], h_s.at[k], h_r.at[k], (ctx, other(head, k, NH))) for k in range(1, NH)
        ])

    def latents_part():
        wait(pending["az"])
        pending["ay"] = start(all_y(dall, 4))
        wait(wq_copies)
        wait(pending["h"])
        mine_rows = pl.ds(pl.multiple_of(head * blk, blk), blk)
        lat_part = dot3(split(hbuf[0]), split(wq[mine_rows]), RHS_T)
        for k in range(1, NH):
            lat_part += dot3(split(hbuf[k]), split(wqr[k]), RHS_T)
        put(lall, lat_part)
        pending["lat"] = start(all_z(lall, 4))

    stages = [dq_to_z, dq_to_all, latents_part]

    for j in range(NZ):
        start(w_y(j))

    todo = [functools.partial(w_sum, j) for j in range(NZ - 1)]
    lax.fori_loop(2 * quarter, 3 * quarter, token_step, 0)
    stages.pop(0)()
    todo.pop(0)()
    lax.fori_loop(3 * quarter, NCH, token_step, 0)
    forward(NCH - 1)
    while stages or todo:
        if stages:
            stages.pop(0)()
        if todo:
            todo.pop(0)()
    wait(att_ay)
    results = start([pltpu.make_async_copy(aall, att_o, res_sem.at[0])])
    wait(pending["lat"])
    lat_ay = start(all_y(lall, 5))
    w_sum(NZ - 1)
    wait(pending["ay"])
    results += start([pltpu.make_async_copy(dall, dq_o, res_sem.at[1])])

    def out_copy(i):
        cols = pl.ds(pl.multiple_of(x * blk, blk), blk)
        return pltpu.make_async_copy(expo.at[0, rows(i), cols], dobs_o.at[rows(i)], out_sem.at[i])

    def finish(i, _):
        cols = pl.ds(pl.multiple_of(x * blk, blk), blk)
        total = expo[0, rows(i), cols]
        for k in range(1, NX):
            second(i, k).wait_recv()
            total += x_recv[k - 1, rows(i)]
        expo[0, rows(i), cols] = total
        out_copy(i).start()
        first(i).wait_send()
        for k in range(1, NX):
            second(i, k).wait_send()
        return 0

    lax.fori_loop(0, NCH, finish, 0)
    wait(lat_ay)
    results += start([pltpu.make_async_copy(lall, dlat_o, res_sem.at[2])])
    dw_mine = dw[pl.ds(z, 1), pl.ds(y, 1)].reshape(r, 2 * W)
    for j in range(NZ - 1):
        w_z(j).wait()
        dw_mine += dw2[1 + j]
    dw2[0] = dw_mine
    results += start([pltpu.make_async_copy(dw2.at[0], dw_o, res_sem.at[3])])

    def drain(i, _):
        out_copy(i).wait()
        return 0

    lax.fori_loop(0, NCH, drain, 0)
    wait(results)


def last_kernel(att, dq, lat, dout, dlat, dobs, dw, dlat_o, dobs_o, dwq_o, dwk_o, dwv_o, dwo_o):
    W = dq.shape[1]
    dwo_o[...] = dot3(split(att[...].T), split(dout[...]))
    dwq_o[...] = dot3(split(lat[...].T), split(dq[...]))
    dobs_o[...] = dobs[...]
    dlat_o[...] = dlat[...]
    dwk_o[...] = dw[:, :W]
    dwv_o[...] = dw[:, W:]


def on_device(nc, nh, latents, observations, w_query, w_key, w_value, w_out, d_out):
    L, D = latents.shape
    T = observations.shape[0]
    W = w_query.shape[1]
    H, blk, la, r = W // DH, D // nh, L // nc, D // nc
    ny = 1 << ((nc.bit_length() - 1) // 2)
    nz, nx = nc // ny, nh // CORES
    tc = min(256, T // 4)
    nch = T // tc
    stat_rows = -(-3 * H // 8) * 8

    def vm(*shape, dtype=F32):
        return pltpu.VMEM(shape, dtype)

    def sems(*shape):
        return pltpu.SemaphoreType.DMA(shape)

    vmem = pl.BlockSpec(memory_space=pltpu.VMEM)
    out = lambda *s: jax.ShapeDtypeStruct(s, F32)
    anywhere = pl.BlockSpec(memory_space=pl.ANY)
    dlat, dobs, dq, dw, att = pl.pallas_call(
        functools.partial(kernel, (nc, nh, ny, tc)),
        out_shape=(out(nz, ny, la, blk), out(T, blk), out(nz, ny, la, W), out(r, 2 * W), out(nz, ny, la, W)),
        in_specs=[vmem, anywhere] + [vmem] * 5,
        out_specs=(anywhere,) * 5,
        scratch_shapes=[
            vm(H, T, L), vm(H, T, L), vm(nch, tc, 2 * W), vm(2, tc, D),
            vm(D, 2 * W, dtype=BF16), vm(D, 2 * W, dtype=BF16),
            vm(H, L, 4 * DH, dtype=BF16), vm(H, L, 4 * DH, dtype=BF16),
            vm(H, L, 2 * DH, dtype=BF16), vm(H, L, 2 * DH, dtype=BF16),
            vm(stat_rows, L), vm(nc, stat_rows, L), vm(W, L),
            vm(T, nx * blk), vm(max(nx - 1, 1), T, blk),
            vm(nz, ny, r, 2 * W), vm(ny, nz, r, 2 * W), vm(nz, r, 2 * W),
            vm(nz, ny, la, W), vm(ny, nz, la, W), vm(nz, la, W),
            vm(nz, ny, la, W), vm(ny, nz, la, W), vm(nz, la, W),
            vm(nz, ny, la, W), vm(nz, ny, la, W), vm(nz, ny, la, blk),
            vm(nh, blk, W), vm(nh, la, W),
            sems(2), sems(nc), sems(nc), sems(nh), sems(nh), sems(nh), sems(nh),
            sems(nch), sems(nch), sems(nx, nch), sems(nx, nch),
            sems(6, ny), sems(6, ny), sems(6, nz), sems(6, nz),
            sems(ny, nz), sems(ny, nz), sems(nz), sems(nz), sems(nch), sems(4),
        ],
        compiler_params=pltpu.CompilerParams(
            collective_id=0, has_side_effects=True, vmem_limit_bytes=63 * 2**20
        ),
        cost_estimate=pl.CostEstimate(flops=3 * 11 * 10**9, bytes_accessed=40 * 2**20, transcendentals=H * T * L),
    )(latents, observations, w_query, w_key, w_value, w_out, d_out)
    steps = 4
    wide = D // steps

    def whole(*shape):
        return pl.BlockSpec(shape, lambda i: (0, 0))

    def by_rows(rows, columns):
        return pl.BlockSpec((rows, columns), lambda i: (i, 0))

    columns = pl.BlockSpec((L, wide), lambda i: (0, i))
    return pl.pallas_call(
        last_kernel,
        grid=(steps,),
        out_shape=(out(L, blk), out(T, blk), out(D, W), out(r, W), out(r, W), out(W, D)),
        in_specs=[
            whole(L, W), whole(L, W), columns, columns,
            by_rows(L // steps, blk), by_rows(T // steps, blk), by_rows(r // steps, 2 * W),
        ],
        out_specs=(
            by_rows(L // steps, blk), by_rows(T // steps, blk), by_rows(wide, W),
            by_rows(r // steps, W), by_rows(r // steps, W), pl.BlockSpec((W, wide), lambda i: (0, i)),
        ),
        compiler_params=pltpu.CompilerParams(vmem_limit_bytes=62 * 2**20),
        cost_estimate=pl.CostEstimate(flops=12 * L * D * W, bytes_accessed=20 * 2**20, transcendentals=0),
    )(att.reshape(L, W), dq.reshape(L, W), latents, d_out, dlat.reshape(L, blk), dobs, dw)


def solution(mesh):
    placed = (
        P(),
        P("ctx", None),
        P(None, "head"),
        P(None, "head"),
        P(None, "head"),
        P("head", None),
        P(),
    )
    return jax.shard_map(
        functools.partial(on_device, mesh.shape["ctx"], mesh.shape["head"]),
        mesh=mesh,
        in_specs=placed,
        out_specs=(
            P(None, "head"),
            P("ctx", "head"),
            P(None, "head"),
            P("ctx", "head"),
            P("ctx", "head"),
            P("head", None),
        ),
        check_vma=False,
    )
```
